32 devices in a mesh: tm: 16 (over z, y, core), space: 2 (over x).
Axes of the slice: x: 2, y: 2, z: 4, core: 2. Of those that a mesh axis runs over, the one named last changes fastest.
Arguments:
- start_states: float32 [16, 3, 4, 256, 256], P('tm', None, 'space'), may hold values from -6 to 6
- wall_normal: bfloat16 [256, 256], replicated, may hold values from -0.375 to 0.375
- spanwise: bfloat16 [256, 256], replicated, may hold values from -0.375 to 0.375
- base_flow: float32 [3, 256], replicated, may hold values from -1.5 to 1.5
Outputs:
- end_state: float32 [16, 3, 4, 256, 256], P('tm', None, 'space')
The draws below stay inside these ranges and needn't reach their ends.
All inputs are finite; a program needn't handle non-finite values.
Results may differ from the reference program's by a relative error of at most 0.0017.
Values sent between devices are 32-bit elements; how exact they have to be, the bound alone decides.
A program may use at most 64 MiB of HBM per device.

```python
from functools import partial
import jax
import jax.numpy as jnp
from jax import lax

Y = 256
Z = 256
TICKS = 2
NX = 4
SLICES = 16


def shard_levels(own_key, dims, cuts, smallest, top_value):
    gain, own = 1.0, jax.random.fold_in(own_key, 6)
    for position, parts in cuts:
        heights = jnp.exp(jax.random.uniform(jax.random.fold_in(own, position), (parts,), jnp.float32, smallest / len(cuts), top_value / len(cuts)))
        gain = gain * jnp.repeat(heights, dims[position] // parts).reshape([-1 if axis == position else 1 for axis in range(len(dims))])
    return gain


def bell_draw(key, shape, width, limit, split=(), held_as=jnp.bfloat16):
    level = shard_levels(key, shape, split, -0.22, 0.18) if split else 1.0
    entries = jax.random.normal(key, shape, jnp.float32) * width * level
    return jnp.minimum(jnp.maximum(entries, -limit), limit).astype(held_as)


def setup_inputs(seed: int = 0) -> dict:
    arg_keys = jax.random.split(jax.random.key(seed), 5)
    return {
        "start_states": bell_draw(arg_keys[0], (SLICES, 3, NX, Y, Z), 1.0, 6.0, ((0, 16), (2, 2)), jnp.float32),
        "wall_normal": bell_draw(arg_keys[1], (Y, Y), Y ** -0.5, 0.375),
        "spanwise": bell_draw(arg_keys[2], (Z, Z), Z ** -0.5, 0.375),
        "base_flow": jnp.clip(jax.random.uniform(arg_keys[3], (3, Y), jnp.float32, -1.5, 1.5), -1.5, 1.5),
    }


step_size = 0.2


def tendency(q, wall_normal, spanwise, base_flow):
    grad_x = 0.5 * (jnp.roll(q, -1, axis=1) - jnp.roll(q, 1, axis=1))
    rounded = q.astype(jnp.bfloat16).astype(jnp.float32)
    grad_y = jnp.einsum("yk,cxkz->cxyz", wall_normal.astype(jnp.float32), rounded, precision=lax.Precision.HIGHEST)
    grad_z = jnp.einsum("cxyk,kz->cxyz", rounded, spanwise.astype(jnp.float32), precision=lax.Precision.HIGHEST)
    velocity = base_flow[:, None, :, None] + q
    return -(velocity[0:1] * grad_x + velocity[1:2] * grad_y + velocity[2:3] * grad_z)


def reference(start_states, wall_normal, spanwise, base_flow):
    evaluate = partial(tendency, wall_normal=wall_normal, spanwise=spanwise, base_flow=base_flow)
    begin = start_states
    finish = start_states
    old_rate = lax.map(evaluate, begin)
    fresh = old_rate
    for tick in range(TICKS):
        if tick > 0:
            fresh = lax.map(evaluate, begin)
        end_rate = lax.map(evaluate, finish)
        finish = begin + step_size * (fresh - old_rate) + 0.5 * step_size * (old_rate + end_rate)
        old_rate = fresh
        if tick < TICKS - 1:
            begin = jnp.concatenate([begin[:1], finish[:-1]], axis=0)
    return finish
```

```python
import functools

import jax
import jax.numpy as jnp
from jax import lax
from jax.experimental import pallas as pl
from jax.experimental.pallas import tpu as pltpu
from jax.sharding import PartitionSpec as P

MESH = pl.DeviceIdType.MESH
ROWS = 32
STEP = 0.2


def layout(count, planes):
    if count == 2 and planes == 2:
        sends = [(0, 0, 1), (1, 1, 1)]
        return sends, 2, lambda e: e + 2 if e < 0 else e - planes
    sends = [(planes - 2, 0, 1), (planes - 1, 1, 1), (0, 2, -1), (1, 3, -1)]
    return sends, 4, lambda e: e + 2 if e < 0 else e - planes + 2


def kernel(ticks_axis, count, start, wall, span, base, out, own, far, gy, gz, u1, gyr, gzr, u1r,
           rate, ub, load_sem, xs, xr, ts, tr, fs, fr):
    comps, planes, height, width = start.shape[1:]
    sends, slots, slot = layout(count, planes)
    t = lax.axis_index("tm")
    x = lax.axis_index("space")
    right, left = lax.rem(x + 1, count), lax.rem(x + count - 1, count)
    has_prev, has_next = t > 0, t < ticks_axis - 1

    load = pltpu.make_async_copy(start.at[0], own.at[0], load_sem)
    load.start()

    barrier = pltpu.get_barrier_semaphore()
    sides = [right] if slots == 2 else [right, left]
    for side in sides:
        pl.semaphore_signal(barrier, inc=1, device_id={"space": side}, device_id_type=MESH)

    @pl.when(has_prev)
    def _():
        pl.semaphore_signal(barrier, inc=1, device_id={"tm": t - 1}, device_id_type=MESH)

    @pl.when(has_next)
    def _():
        pl.semaphore_signal(barrier, inc=1, device_id={"tm": t + 1}, device_id_type=MESH)

    pl.semaphore_wait(barrier, len(sides) + has_prev.astype(jnp.int32) + has_next.astype(jnp.int32))

    def across(c, i):
        p, k, way = sends[i]
        return pltpu.make_async_remote_copy(
            src_ref=start.at[0, c, p], dst_ref=far.at[0, c, k], send_sem=xs.at[c, k], recv_sem=xr.at[c, k],
            device_id={"space": right if way == 1 else left}, device_id_type=MESH)

    def onward(c):
        return pltpu.make_async_remote_copy(
            src_ref=start.at[0, c], dst_ref=own.at[1, c], send_sem=ts.at[c], recv_sem=tr.at[c],
            device_id={"tm": t + 1}, device_id_type=MESH)

    def forward(c, k):
        return pltpu.make_async_remote_copy(
            src_ref=far.at[0, c, k], dst_ref=far.at[1, c, k], send_sem=fs.at[c, k], recv_sem=fr.at[c, k],
            device_id={"tm": t + 1}, device_id_type=MESH)

    for c in range(comps):
        for i in range(len(sends)):
            across(c, i).start()

    @pl.when(has_next)
    def _():
        for c in range(comps):
            onward(c).start()

    for c in range(comps):
        ub[c] = jnp.broadcast_to(base[c][None, :], (width, height)).T

    def grads(src, to_y, to_z):
        rounded = src[...].astype(jnp.bfloat16)
        to_y[...] = jnp.dot(wall[...], rounded, preferred_element_type=jnp.float32)
        to_z[...] = jnp.dot(rounded, span[...], preferred_element_type=jnp.float32)

    def plane(g, c, e):
        return own.at[g, c, e] if 0 <= e < planes else far.at[g, c, slot(e)]

    def after(g, c, e):
        return u1.at[g, c, e] if 0 <= e < planes else u1r.at[g, c, 0 if e < 0 else 1]

    def blocks(body):
        @pl.loop(0, height // ROWS)
        def _(b):
            body(pl.ds(pl.multiple_of(b * ROWS, ROWS), ROWS))

    def first(g):
        for c in range(comps):
            for p in range(planes):
                grads(own.at[g, c, p], gy.at[g, c, p], gz.at[g, c, p])

    def second(g, c):
        for i, e in enumerate((-1, planes)):
            grads(plane(g, c, e), gyr.at[g, c, i], gzr.at[g, c, i])
        for p in range(planes):
            def body(r):
                gx = 0.5 * (plane(g, c, p + 1)[r] - plane(g, c, p - 1)[r])
                f = -((ub[0, r] + own[g, 0, p, r]) * gx + (ub[1, r] + own[g, 1, p, r]) * gy[g, c, p, r]
                      + (ub[2, r] + own[g, 2, p, r]) * gz[g, c, p, r])
                if g == 0:
                    rate[c, p, r] = f
                u1[g, c, p, r] = own[g, c, p, r] + STEP * f
            blocks(body)
            grads(u1.at[g, c, p], gy.at[g, c, p], gz.at[g, c, p])

    def third(g):
        for i, e in enumerate((-1, planes)):
            def body(r):
                v = [ub[d, r] + plane(g, d, e)[r] for d in range(3)]
                for c in range(comps):
                    gx = 0.5 * (plane(g, c, e + 1)[r] - plane(g, c, e - 1)[r])
                    f = -(v[0] * gx + v[1] * gyr[g, c, i, r] + v[2] * gzr[g, c, i, r])
                    u1r[g, c, i, r] = plane(g, c, e)[r] + STEP * f
            blocks(body)

    def fourth(g, finish):
        for p in range(planes):
            def body(r):
                v = [ub[d, r] + u1[g, d, p, r] for d in range(3)]
                for c in range(comps):
                    gx = 0.5 * (after(g, c, p + 1)[r] - after(g, c, p - 1)[r])
                    finish(c, p, r, -(v[0] * gx + v[1] * gy[g, c, p, r] + v[2] * gz[g, c, p, r]))
            blocks(body)

    def own_part(c, p, r, f):
        rate[c, p, r] = 0.5 * STEP * (f - rate[c, p, r])

    def alone(c, p, r, f):
        out[0, c, p, r] = u1[0, c, p, r] + 0.5 * STEP * (f - rate[c, p, r])

    def joined(c, p, r, f):
        out[0, c, p, r] = u1[1, c, p, r] + STEP * f + rate[c, p, r]

    def arrive(c):
        for _, k, _ in sends:
            i = [s[1] for s in sends].index(k)
            across(c, i).wait_recv()

            @pl.when(has_next)
            def _():
                forward(c, k).start()

    def prev_arrive(c):
        for _, k, _ in sends:
            forward(c, k).wait_recv()

    load.wait()
    first(0)
    arrive(0)
    second(0, 0)
    arrive(1)
    second(0, 1)

    @pl.when(has_prev)
    def _():
        for c in range(comps):
            onward(c).wait_recv()
        first(1)
        prev_arrive(0)
        second(1, 0)

    arrive(2)
    second(0, 2)
    third(0)

    @pl.when(t == 0)
    def _():
        fourth(0, alone)

    @pl.when(has_prev)
    def _():
        fourth(0, own_part)
        for c in range(1, comps):
            prev_arrive(c)
            second(1, c)
        third(1)
        fourth(1, joined)

    for c in range(comps):
        for i in range(len(sends)):
            across(c, i).wait_send()

    @pl.when(has_next)
    def _():
        for c in range(comps):
            onward(c).wait_send()
            for _, k, _ in sends:
                forward(c, k).wait_send()


def local(ticks_axis, count, start_states, wall_normal, spanwise, base_flow):
    _, comps, planes, height, width = start_states.shape
    slots = layout(count, planes)[1]
    vmem = lambda *shape: pltpu.VMEM(shape, jnp.float32)
    state = lambda *lead: vmem(*lead, height, width)
    return pl.pallas_call(
        functools.partial(kernel, ticks_axis, count),
        out_shape=jax.ShapeDtypeStruct(start_states.shape, jnp.float32),
        in_specs=[pl.BlockSpec(memory_space=pl.ANY)] + [pl.BlockSpec(memory_space=pltpu.VMEM)] * 3,
        out_specs=pl.BlockSpec(memory_space=pltpu.VMEM),
        scratch_shapes=[
            state(2, comps, planes), state(2, comps, slots),
            state(2, comps, planes), state(2, comps, planes), state(2, comps, planes),
            state(2, comps, 2), state(2, comps, 2), state(2, comps, 2),
            state(comps, planes), state(3),
            pltpu.SemaphoreType.DMA,
            pltpu.SemaphoreType.DMA((comps, slots)), pltpu.SemaphoreType.DMA((comps, slots)),
            pltpu.SemaphoreType.DMA((comps,)), pltpu.SemaphoreType.DMA((comps,)),
            pltpu.SemaphoreType.DMA((comps, slots)), pltpu.SemaphoreType.DMA((comps, slots)),
        ],
        compiler_params=pltpu.CompilerParams(
            collective_id=0, has_side_effects=True, vmem_limit_bytes=50 * 1024 * 1024),
    )(start_states, wall_normal, spanwise, base_flow)


def solution(mesh):
    return jax.shard_map(
        functools.partial(local, mesh.shape["tm"], mesh.shape["space"]),
        mesh=mesh,
        in_specs=(P("tm", None, "space", None, None), P(), P(), P()),
        out_specs=P("tm", None, "space", None, None),
        check_vma=False,
    )
```

```python
import functools

import jax
import jax.numpy as jnp
from jax import lax
from jax.experimental import pallas as pl
from jax.experimental.pallas import tpu as pltpu
from jax.sharding import PartitionSpec as P

MESH = pl.DeviceIdType.MESH
ROWS = 32
STEP = 0.2
PIECES = (1, 1, 4)


def layout(count, planes):
    if count == 2 and planes == 2:
        sends = [(0, 0, 1), (1, 1, 1)]
        return sends, 2, lambda e: e + 2 if e < 0 else e - planes
    sends = [(planes - 2, 0, 1), (planes - 1, 1, 1), (0, 2, -1), (1, 3, -1)]
    return sends, 4, lambda e: e + 2 if e < 0 else e - planes + 2


def kernel(ticks_axis, count, start, wall_hbm, span_hbm, base_hbm, out, wall, span, base, own, far, gy, gz, u1, gyr, gzr, u1r,
           rate, ub, load_sem, xs, xr, ts, tr, fs, fr):
    comps, planes, height, width = start.shape[1:]
    sends, slots, slot = layout(count, planes)
    edges = (-1, planes)
    t = lax.axis_index("tm")
    x = lax.axis_index("space")
    right, left = lax.rem(x + 1, count), lax.rem(x + count - 1, count)
    has_prev, has_next = t > 0, t < ticks_axis - 1

    loads = [pltpu.make_async_copy(src, dst, load_sem.at[i]) for i, (src, dst) in enumerate(
        ((base_hbm, base), (wall_hbm, wall), (span_hbm, span), (start.at[0], own.at[0])))]
    for load in loads:
        load.start()

    barrier = pltpu.get_barrier_semaphore()
    sides = [right] if slots == 2 else [right, left]
    for side in sides:
        pl.semaphore_signal(barrier, inc=1, device_id={"space": side}, device_id_type=MESH)

    @pl.when(has_prev)
    def _():
        pl.semaphore_signal(barrier, inc=1, device_id={"tm": t - 1}, device_id_type=MESH)

    @pl.when(has_next)
    def _():
        pl.semaphore_signal(barrier, inc=1, device_id={"tm": t + 1}, device_id_type=MESH)

    pl.semaphore_wait(barrier, len(sides) + has_prev.astype(jnp.int32) + has_next.astype(jnp.int32))

    def piece(c, j):
        rows = height // PIECES[c]
        return pl.ds(j * rows, rows)

    def across(c, i, j):
        p, k, way = sends[i]
        r = piece(c, j)
        return pltpu.make_async_remote_copy(
            src_ref=start.at[0, c, p, r], dst_ref=far.at[0, c, k, r],
            send_sem=xs.at[c, k, j], recv_sem=xr.at[c, k, j],
            device_id={"space": right if way == 1 else left}, device_id_type=MESH)

    def onward(c):
        return pltpu.make_async_remote_copy(
            src_ref=start.at[0, c], dst_ref=own.at[1, c], send_sem=ts.at[c], recv_sem=tr.at[c],
            device_id={"tm": t + 1}, device_id_type=MESH)

    def forward(c, k, j):
        r = piece(c, j)
        return pltpu.make_async_remote_copy(
            src_ref=far.at[0, c, k, r], dst_ref=far.at[1, c, k, r],
            send_sem=fs.at[c, k, j], recv_sem=fr.at[c, k, j],
            device_id={"tm": t + 1}, device_id_type=MESH)

    for c in range(comps):
        for i in range(len(sends)):
            for j in range(PIECES[c]):
                across(c, i, j).start()

    @pl.when(has_next)
    def _():
        for c in range(comps):
            onward(c).start()

    loads[0].wait()
    for c in range(comps):
        ub[c] = jnp.broadcast_to(base[c][None, :], (width, height)).T

    def grads(src, to_y, to_z):
        rounded = src[...].astype(jnp.bfloat16)
        to_y[...] = jnp.dot(wall[...], rounded, preferred_element_type=jnp.float32)
        to_z[...] = jnp.dot(rounded, span[...], preferred_element_type=jnp.float32)

    def plane(g, c, e):
        return own.at[g, c, e] if 0 <= e < planes else far.at[g, c, slot(e)]

    def after(g, c, e):
        return u1.at[g, c, e] if 0 <= e < planes else u1r.at[g, c, 0 if e < 0 else 1]

    def blocks(body):
        @pl.loop(0, height // ROWS)
        def _(b):
            body(pl.ds(pl.multiple_of(b * ROWS, ROWS), ROWS))

    def first(g):
        for c in range(comps):
            for p in range(planes):
                grads(own.at[g, c, p], gy.at[g, c, p], gz.at[g, c, p])

    def far_grads(g, c, i):
        grads(plane(g, c, edges[i]), gyr.at[g, c, i], gzr.at[g, c, i])

    def advance(g, c, p):
        def body(r):
            gx = 0.5 * (plane(g, c, p + 1)[r] - plane(g, c, p - 1)[r])
            f = -((ub[0, r] + own[g, 0, p, r]) * gx + (ub[1, r] + own[g, 1, p, r]) * gy[g, c, p, r]
                  + (ub[2, r] + own[g, 2, p, r]) * gz[g, c, p, r])
            if g == 0:
                rate[c, p, r] = f
            u1[g, c, p, r] = own[g, c, p, r] + STEP * f
        blocks(body)
        grads(u1.at[g, c, p], gy.at[g, c, p], gz.at[g, c, p])

    def far_advance(g, cs, i):
        e = edges[i]

        def body(r):
            v = [ub[d, r] + plane(g, d, e)[r] for d in range(3)]
            for c in cs:
                gx = 0.5 * (plane(g, c, e + 1)[r] - plane(g, c, e - 1)[r])
                f = -(v[0] * gx + v[1] * gyr[g, c, i, r] + v[2] * gzr[g, c, i, r])
                u1r[g, c, i, r] = plane(g, c, e)[r] + STEP * f
        blocks(body)

    def finish(g, cs, p, write):
        def body(r):
            v = [ub[d, r] + u1[g, d, p, r] for d in range(3)]
            for c in cs:
                gx = 0.5 * (after(g, c, p + 1)[r] - after(g, c, p - 1)[r])
                write(c, p, r, -(v[0] * gx + v[1] * gy[g, c, p, r] + v[2] * gz[g, c, p, r]))
        blocks(body)

    def own_part(c, p, r, f):
        rate[c, p, r] = 0.5 * STEP * (f - rate[c, p, r])

    def alone(c, p, r, f):
        out[0, c, p, r] = u1[0, c, p, r] + 0.5 * STEP * (f - rate[c, p, r])

    def joined(c, p, r, f):
        out[0, c, p, r] = u1[1, c, p, r] + STEP * f + rate[c, p, r]

    chunks = [(c, k) for c in range(comps) for _, k, _ in sends]
    foreign = lambda c, *es: {(c, slot(e)) for e in es if not 0 <= e < planes}
    needs_far = lambda c, i: set().union(
        foreign(c, edges[i] - 1, edges[i] + 1), *(foreign(d, edges[i]) for d in range(comps)))
    needs_own = lambda c, p: foreign(c, p - 1, p + 1)
    needs_end = lambda c, p: set().union(
        *(needs_own(d, p) for d in range(comps)), *(needs_own(c, q) for q in (p - 1, p + 1) if 0 <= q < planes),
        *(needs_far(c, i) for i, e in enumerate(edges) if abs(e - p) == 1))
    last = lambda needs: max([chunks.index(n) for n in needs], default=0)
    ready = lambda n, of, j: [c for c in range(comps) if last(of(c, j)) == n]

    def work(g, n, write):
        c, k = chunks[n]
        for i, e in enumerate(edges):
            if slot(e) == k:
                far_grads(g, c, i)
        for p in range(planes):
            for d in ready(n, needs_own, p):
                advance(g, d, p)
        for i in range(2):
            if ready(n, needs_far, i):
                far_advance(g, ready(n, needs_far, i), i)
        for p in range(planes):
            if ready(n, needs_end, p):
                if write is None:
                    pl.when(t == 0)(lambda: finish(g, ready(n, needs_end, p), p, alone))
                    pl.when(has_prev)(lambda: finish(g, ready(n, needs_end, p), p, own_part))
                else:
                    finish(g, ready(n, needs_end, p), p, write)

    def arrive(n):
        c, k = chunks[n]
        i = [s[1] for s in sends].index(k)
        for j in range(PIECES[c]):
            across(c, i, j).wait_recv()

            @pl.when(has_next)
            def _():
                forward(c, k, j).start()
        work(0, n, None)

    def prev_arrive(n):
        c, k = chunks[n]
        for j in range(PIECES[c]):
            forward(c, k, j).wait_recv()
        work(1, n, joined)

    for load in loads[1:]:
        load.wait()
    first(0)
    each = len(sends)
    for n in range(2 * each):
        arrive(n)

    @pl.when(has_prev)
    def _():
        for c in range(comps):
            onward(c).wait_recv()
        first(1)
        for n in range(each):
            prev_arrive(n)

    for n in range(2 * each, 3 * each - 1):
        arrive(n)

    @pl.when(has_prev)
    def _():
        for n in range(each, 3 * each - 1):
            prev_arrive(n)

    arrive(3 * each - 1)

    @pl.when(has_prev)
    def _():
        prev_arrive(3 * each - 1)

    for c in range(comps):
        for i in range(len(sends)):
            for j in range(PIECES[c]):
                across(c, i, j).wait_send()

    @pl.when(has_next)
    def _():
        for c in range(comps):
            onward(c).wait_send()
            for _, k, _ in sends:
                for j in range(PIECES[c]):
                    forward(c, k, j).wait_send()


def local(ticks_axis, count, start_states, wall_normal, spanwise, base_flow):
    _, comps, planes, height, width = start_states.shape
    slots = layout(count, planes)[1]
    vmem = lambda *shape: pltpu.VMEM(shape, jnp.float32)
    state = lambda *lead: vmem(*lead, height, width)
    return pl.pallas_call(
        functools.partial(kernel, ticks_axis, count),
        out_shape=jax.ShapeDtypeStruct(start_states.shape, jnp.float32),
        in_specs=[pl.BlockSpec(memory_space=pltpu.HBM)] * 4,
        out_specs=pl.BlockSpec(memory_space=pltpu.VMEM),
        scratch_shapes=[
            pltpu.VMEM(wall_normal.shape, wall_normal.dtype), pltpu.VMEM(spanwise.shape, spanwise.dtype),
            pltpu.VMEM(base_flow.shape, base_flow.dtype),
            state(2, comps, planes), state(2, comps, slots),
            state(2, comps, planes), state(2, comps, planes), state(2, comps, planes),
            state(2, comps, 2), state(2, comps, 2), state(2, comps, 2),
            state(comps, planes), state(3),
            pltpu.SemaphoreType.DMA((4,)),
            pltpu.SemaphoreType.DMA((comps, slots, max(PIECES))), pltpu.SemaphoreType.DMA((comps, slots, max(PIECES))),
            pltpu.SemaphoreType.DMA((comps,)), pltpu.SemaphoreType.DMA((comps,)),
            pltpu.SemaphoreType.DMA((comps, slots, max(PIECES))), pltpu.SemaphoreType.DMA((comps, slots, max(PIECES))),
        ],
        compiler_params=pltpu.CompilerParams(
            collective_id=0, has_side_effects=True, vmem_limit_bytes=63 * 1024 * 1024),
    )(start_states, wall_normal, spanwise, base_flow)


def solution(mesh):
    return jax.shard_map(
        functools.partial(local, mesh.shape["tm"], mesh.shape["space"]),
        mesh=mesh,
        in_specs=(P("tm", None, "space", None, None), P(), P(), P()),
        out_specs=P("tm", None, "space", None, None),
        check_vma=False,
    )
```

```python
import functools

import jax
import jax.numpy as jnp
from jax import lax
from jax.experimental import pallas as pl
from jax.experimental.pallas import tpu as pltpu
from jax.sharding import PartitionSpec as P

MESH = pl.DeviceIdType.MESH
ROWS = 64
STEP = 0.2
PIECES = (1, 1, 4)


def layout(count, planes):
    if count == 2 and planes == 2:
        sends = [(0, 0, 1), (1, 1, 1)]
        return sends, 2, lambda e: e + 2 if e < 0 else e - planes
    sends = [(planes - 2, 0, 1), (planes - 1, 1, 1), (0, 2, -1), (1, 3, -1)]
    return sends, 4, lambda e: e + 2 if e < 0 else e - planes + 2


def kernel(ticks_axis, count, start, wall_hbm, span_hbm, base_hbm, out, wall, span, base, own, far, gy, gz, u1, gyr, gzr, u1r,
           rate, ub, load_sem, xs, xr, ts, tr, fs, fr):
    comps, planes, height, width = start.shape[1:]
    sends, slots, slot = layout(count, planes)
    edges = (-1, planes)
    t = lax.axis_index("tm")
    x = lax.axis_index("space")
    right, left = lax.rem(x + 1, count), lax.rem(x + count - 1, count)
    has_prev, has_next = t > 0, t < ticks_axis - 1

    loads = [pltpu.make_async_copy(src, dst, load_sem.at[i]) for i, (src, dst) in enumerate(
        ((base_hbm, base), (wall_hbm, wall), (span_hbm, span), (start.at[0], own.at[0])))]
    for load in loads:
        load.start()

    barrier = pltpu.get_barrier_semaphore()
    sides = [right] if slots == 2 else [right, left]
    for side in sides:
        pl.semaphore_signal(barrier, inc=1, device_id={"space": side}, device_id_type=MESH)

    @pl.when(has_prev)
    def _():
        pl.semaphore_signal(barrier, inc=1, device_id={"tm": t - 1}, device_id_type=MESH)

    @pl.when(has_next)
    def _():
        pl.semaphore_signal(barrier, inc=1, device_id={"tm": t + 1}, device_id_type=MESH)

    pl.semaphore_wait(barrier, len(sides) + has_prev.astype(jnp.int32) + has_next.astype(jnp.int32))

    def piece(c, j):
        rows = height // PIECES[c]
        return pl.ds(j * rows, rows)

    def across(c, i, j):
        p, k, way = sends[i]
        r = piece(c, j)
        return pltpu.make_async_remote_copy(
            src_ref=start.at[0, c, p, r], dst_ref=far.at[0, c, k, r],
            send_sem=xs.at[c, k, j], recv_sem=xr.at[c, k, j],
            device_id={"space": right if way == 1 else left}, device_id_type=MESH)

    def onward(c):
        return pltpu.make_async_remote_copy(
            src_ref=start.at[0, c], dst_ref=own.at[1, c], send_sem=ts.at[c], recv_sem=tr.at[c],
            device_id={"tm": t + 1}, device_id_type=MESH)

    def forward(c, k, j):
        r = piece(c, j)
        return pltpu.make_async_remote_copy(
            src_ref=far.at[0, c, k, r], dst_ref=far.at[1, c, k, r],
            send_sem=fs.at[c, k, j], recv_sem=fr.at[c, k, j],
            device_id={"tm": t + 1}, device_id_type=MESH)

    for c in range(comps):
        for i in range(len(sends)):
            for j in range(PIECES[c]):
                across(c, i, j).start()

    @pl.when(has_next)
    def _():
        for c in range(comps):
            onward(c).start()

    loads[0].wait()
    for c in range(comps):
        ub[c] = jnp.broadcast_to(base[c][None, :], (width, height)).T

    def grads(src, to_y, to_z):
        rounded = src[...].astype(jnp.bfloat16)
        to_y[...] = jnp.dot(wall[...], rounded, preferred_element_type=jnp.float32)
        to_z[...] = jnp.dot(rounded, span[...], preferred_element_type=jnp.float32)

    def plane(g, c, e):
        return own.at[g, c, e] if 0 <= e < planes else far.at[g, c, slot(e)]

    def after(g, c, e):
        return u1.at[g, c, e] if 0 <= e < planes else u1r.at[g, c, 0 if e < 0 else 1]

    def blocks(body):
        @pl.loop(0, height // ROWS)
        def _(b):
            body(pl.ds(pl.multiple_of(b * ROWS, ROWS), ROWS))

    def first(g):
        for c in range(comps):
            for p in range(planes):
                grads(own.at[g, c, p], gy.at[g, c, p], gz.at[g, c, p])

    def far_grads(g, c, i):
        grads(plane(g, c, edges[i]), gyr.at[g, c, i], gzr.at[g, c, i])

    def advance(g, c, p):
        def body(r):
            gx = 0.5 * (plane(g, c, p + 1)[r] - plane(g, c, p - 1)[r])
            f = -((ub[0, r] + own[g, 0, p, r]) * gx + (ub[1, r] + own[g, 1, p, r]) * gy[g, c, p, r]
                  + (ub[2, r] + own[g, 2, p, r]) * gz[g, c, p, r])
            if g == 0:
                rate[c, p, r] = f
            u1[g, c, p, r] = own[g, c, p, r] + STEP * f
        blocks(body)
        grads(u1.at[g, c, p], gy.at[g, c, p], gz.at[g, c, p])

    def far_advance(g, cs, i):
        e = edges[i]

        def body(r):
            v = [ub[d, r] + plane(g, d, e)[r] for d in range(3)]
            for c in cs:
                gx = 0.5 * (plane(g, c, e + 1)[r] - plane(g, c, e - 1)[r])
                f = -(v[0] * gx + v[1] * gyr[g, c, i, r] + v[2] * gzr[g, c, i, r])
                u1r[g, c, i, r] = plane(g, c, e)[r] + STEP * f
        blocks(body)

    def finish(g, cs, p, write):
        def body(r):
            v = [ub[d, r] + u1[g, d, p, r] for d in range(3)]
            for c in cs:
                gx = 0.5 * (after(g, c, p + 1)[r] - after(g, c, p - 1)[r])
                write(c, p, r, -(v[0] * gx + v[1] * gy[g, c, p, r] + v[2] * gz[g, c, p, r]))
        blocks(body)

    def own_part(c, p, r, f):
        rate[c, p, r] = 0.5 * STEP * (f - rate[c, p, r])

    def alone(c, p, r, f):
        out[0, c, p, r] = u1[0, c, p, r] + 0.5 * STEP * (f - rate[c, p, r])

    def joined(c, p, r, f):
        out[0, c, p, r] = u1[1, c, p, r] + STEP * f + rate[c, p, r]

    chunks = [(c, k) for c in range(comps) for _, k, _ in sends]
    foreign = lambda c, *es: {(c, slot(e)) for e in es if not 0 <= e < planes}
    needs_far = lambda c, i: set().union(
        foreign(c, edges[i] - 1, edges[i] + 1), *(foreign(d, edges[i]) for d in range(comps)))
    needs_own = lambda c, p: foreign(c, p - 1, p + 1)
    needs_end = lambda c, p: set().union(
        *(needs_own(d, p) for d in range(comps)), *(needs_own(c, q) for q in (p - 1, p + 1) if 0 <= q < planes),
        *(needs_far(c, i) for i, e in enumerate(edges) if abs(e - p) == 1))
    last = lambda needs: max([chunks.index(n) for n in needs], default=0)
    ready = lambda n, of, j: [c for c in range(comps) if last(of(c, j)) == n]

    def work(g, n, write):
        c, k = chunks[n]
        for i, e in enumerate(edges):
            if slot(e) == k:
                far_grads(g, c, i)
        for p in range(planes):
            for d in ready(n, needs_own, p):
                advance(g, d, p)
        for i in range(2):
            if ready(n, needs_far, i):
                far_advance(g, ready(n, needs_far, i), i)
        for p in range(planes):
            if ready(n, needs_end, p):
                if write is None:
                    pl.when(t == 0)(lambda: finish(g, ready(n, needs_end, p), p, alone))
                    pl.when(has_prev)(lambda: finish(g, ready(n, needs_end, p), p, own_part))
                else:
                    finish(g, ready(n, needs_end, p), p, write)

    def arrive(n):
        c, k = chunks[n]
        i = [s[1] for s in sends].index(k)
        for j in range(PIECES[c]):
            across(c, i, j).wait_recv()

            @pl.when(has_next)
            def _():
                forward(c, k, j).start()
        work(0, n, None)

    def prev_arrive(n):
        c, k = chunks[n]
        for j in range(PIECES[c]):
            forward(c, k, j).wait_recv()
        work(1, n, joined)

    for load in loads[1:]:
        load.wait()
    first(0)
    each = len(sends)
    for n in range(2 * each):
        arrive(n)

    @pl.when(has_prev)
    def _():
        for c in range(comps):
            onward(c).wait_recv()
        first(1)
        for n in range(each):
            prev_arrive(n)

    for n in range(2 * each, 3 * each - 1):
        arrive(n)

    @pl.when(has_prev)
    def _():
        for n in range(each, 3 * each - 1):
            prev_arrive(n)

    arrive(3 * each - 1)

    @pl.when(has_prev)
    def _():
        prev_arrive(3 * each - 1)

    for c in range(comps):
        for i in range(len(sends)):
            for j in range(PIECES[c]):
                across(c, i, j).wait_send()

    @pl.when(has_next)
    def _():
        for c in range(comps):
            onward(c).wait_send()
            for _, k, _ in sends:
                for j in range(PIECES[c]):
                    forward(c, k, j).wait_send()


def local(ticks_axis, count, start_states, wall_normal, spanwise, base_flow):
    _, comps, planes, height, width = start_states.shape
    slots = layout(count, planes)[1]
    vmem = lambda *shape: pltpu.VMEM(shape, jnp.float32)
    state = lambda *lead: vmem(*lead, height, width)
    return pl.pallas_call(
        functools.partial(kernel, ticks_axis, count),
        out_shape=pltpu.VMEM(start_states.shape, jnp.float32),
        in_specs=[pl.BlockSpec(memory_space=pltpu.HBM)] * 4,
        out_specs=pl.BlockSpec(memory_space=pltpu.VMEM),
        scratch_shapes=[
            pltpu.VMEM(wall_normal.shape, wall_normal.dtype), pltpu.VMEM(spanwise.shape, spanwise.dtype),
            pltpu.VMEM(base_flow.shape, base_flow.dtype),
            state(2, comps, planes), state(2, comps, slots),
            state(2, comps, planes), state(2, comps, planes), state(2, comps, planes),
            state(2, comps, 2), state(2, comps, 2), state(2, comps, 2),
            state(comps, planes), state(3),
            pltpu.SemaphoreType.DMA((4,)),
            pltpu.SemaphoreType.DMA((comps, slots, max(PIECES))), pltpu.SemaphoreType.DMA((comps, slots, max(PIECES))),
            pltpu.SemaphoreType.DMA((comps,)), pltpu.SemaphoreType.DMA((comps,)),
            pltpu.SemaphoreType.DMA((comps, slots, max(PIECES))), pltpu.SemaphoreType.DMA((comps, slots, max(PIECES))),
        ],
        compiler_params=pltpu.CompilerParams(
            collective_id=0, has_side_effects=True, vmem_limit_bytes=52 * 1024 * 1024),
    )(*(pltpu.with_memory_space_constraint(v, pltpu.HBM) for v in (start_states, wall_normal, spanwise, base_flow)))


def solution(mesh):
    return jax.shard_map(
        functools.partial(local, mesh.shape["tm"], mesh.shape["space"]),
        mesh=mesh,
        in_specs=(P("tm", None, "space", None, None), P(), P(), P()),
        out_specs=P("tm", None, "space", None, None),
        check_vma=False,
    )
```
